32 devices in a mesh: dom: 8 (over z, x), rep: 4 (over y, core).
Axes of the slice: x: 2, y: 2, z: 4, core: 2. Of those that a mesh axis runs over, the one named last changes fastest.
Arguments:
- feats: bfloat16 [128, 32768], P('rep', 'dom'), may hold values from -6 to 6
- grad_out: bfloat16 [128, 32768], P('rep', 'dom'), may hold values from -6 to 6
- w_self: bfloat16 [128, 128], replicated, may hold values from -0.5 to 0.5
- w_neigh: bfloat16 [128, 128], replicated, may hold values from -0.5 to 0.5
- bias: float32 [128], replicated, may hold values from -3 to 3
- requests: int32 [8, 8], P('dom'), may hold values from -1 to 31, as said below
- cross_peer: int32 [768], P('dom'), may hold values from 0 to 7, as said below
- cross_block: int32 [768], P('dom'), may hold values from 0 to 31
- cross_count: int32 [8], P('dom'), may hold values from 1 to 96, as said below
- cross_w: bfloat16 [768, 128, 128], P('dom'), may hold values from -0.25 to 0.25
- inner_src: int32 [128], P('dom'), may hold values from 0 to 31
- inner_dst: int32 [128], P('dom'), may hold values from 0 to 31
- inner_w: bfloat16 [128, 128, 128], P('dom'), may hold values from -0.25 to 0.25
Outputs:
- activated: bfloat16 [128, 32768], P('rep', 'dom')
- d_feats: bfloat16 [128, 32768], P('rep', 'dom')
- grad_self: float32 [128, 128], P('rep')
- grad_neigh: float32 [128, 128], P('rep')
- grad_bias: float32 [128], P('rep')
The draws below stay inside these ranges and needn't reach their ends.
Inputs may be any that keep to these rules, and one draw needn't show every extreme that they name: requests[p, q] >= 0 exactly when some cross tile of partition q names p as its peer; requests[p, p] = -1. `cross_peer`: every cross tile, live or not, names a peer p with requests[p, own partition] >= 0, never its own partition. `cross_count`: every peer that a partition's tiles name is named by one of its live tiles.
All inputs are finite; a program needn't handle non-finite values.
Results may differ from the reference program's by a relative error of at most 0.0058.
Values may be sent and summed in bfloat16 or wider, within the bound.
A program may use at most 64 MiB of HBM per device.

```python
import math
import jax
import jax.numpy as jnp
from jax import lax

F = 128
HID = 128
BLK = 128
NB = 32
CT = 96
IT = 16
NODES = 32768
CROSS = 768
INNER = 128
N_DOM = 8


def draw_plan(key):
    keys = jax.random.split(key, 6)
    parts_idx = jnp.arange(N_DOM, dtype=jnp.int32)
    shifts = jax.random.randint(keys[0], (N_DOM,), 0, 2)
    busiest = jax.random.randint(keys[1], (), 0, N_DOM)
    shifts = jnp.where(parts_idx == busiest, 0, shifts)
    counts = jnp.right_shift(jnp.full((N_DOM,), CT, jnp.int32), shifts.astype(jnp.int32))
    reading = jnp.maximum(1, jnp.minimum(counts, N_DOM - 1))
    offsets = jax.vmap(lambda sub: jax.random.permutation(sub, N_DOM - 1))(jax.random.split(keys[2], N_DOM)) + 1
    offsets = offsets.astype(jnp.int32)
    chosen = jax.random.randint(keys[3], (N_DOM, CT), 0, reading[:, None])
    slot_idx = jnp.arange(CT, dtype=jnp.int32)[None, :]
    rank_k = jnp.where(slot_idx < reading[:, None], slot_idx, chosen)
    far_part = (parts_idx[:, None] + jnp.take_along_axis(offsets, rank_k, axis=1)) % N_DOM
    placed = jnp.argsort(offsets, axis=1).astype(jnp.int32)
    shift_pq = (parts_idx[None, :] - parts_idx[:, None]) % N_DOM
    safe_shift = jnp.maximum(shift_pq - 1, 0)
    order_pq = jnp.take_along_axis(placed, safe_shift, axis=1)
    is_read = (shift_pq != 0) & (order_pq < reading[:, None])
    wanted_block = jax.random.randint(keys[4], (N_DOM, N_DOM), 0, NB)
    read_table = jnp.where(is_read, wanted_block, -1)
    near_block = jax.random.randint(keys[5], (N_DOM, CT), 0, NB)
    return (read_table.T, far_part.reshape(-1), near_block.reshape(-1), counts)


def draw_requests(key, part):
    shared = draw_plan(key)
    return shared[0].astype(jnp.int32)


def draw_cross_peer(key, part):
    shared = draw_plan(key)
    return shared[1].astype(jnp.int32)


def draw_cross_block(key, part):
    shared = draw_plan(key)
    return shared[2].astype(jnp.int32)


def draw_cross_count(key, part):
    shared = draw_plan(key)
    return shared[3].astype(jnp.int32)


def plant(values, stream_key, least, high):
    extent = values.shape
    spot = [jax.random.randint(jax.random.fold_in(stream_key, axis), (), 0, extent[axis]) for axis in range(len(extent))]
    values = values.at[tuple(spot)].set(least)
    longest = extent.index(max(extent))
    spot[longest] = (spot[longest] + 1) % extent[longest]
    return values.at[tuple(spot)].set(high)


def block_levels(key, extent, pieces, least, high):
    def one(dim, parts):
        steps = jax.random.uniform(jax.random.fold_in(jax.random.fold_in(key, 6), dim), (parts,), jnp.float32, least / len(pieces), high / len(pieces))
        return jnp.repeat(jnp.exp(steps), extent[dim] // parts).reshape((-1,) + (1,) * (len(extent) - dim - 1))

    loudness = one(*pieces[0])
    for cut in pieces[1:]:
        loudness = loudness * one(*cut)
    return loudness


def scatter_about(own_key, extent, scale, bound, cuts=(), kind=jnp.bfloat16):
    result = jax.random.normal(own_key, extent, jnp.float32) * scale
    if len(cuts) > 0:
        result = block_levels(own_key, extent, cuts, -0.22, 0.18) * result
    return jnp.clip(result, min=-bound, max=bound).astype(kind)


def setup_inputs(seed: int = 0) -> dict:
    arg_keys = jax.random.split(jax.random.key(seed), 14)
    return {
        "feats": scatter_about(arg_keys[0], (F, NODES), 1.0, 6.0, ((0, 4), (1, 8))),
        "grad_out": scatter_about(arg_keys[1], (HID, NODES), 1.0, 6.0, ((0, 4), (1, 8))),
        "w_self": scatter_about(arg_keys[2], (F, HID), F ** -0.5, 0.5),
        "w_neigh": scatter_about(arg_keys[3], (F, HID), F ** -0.5, 0.5),
        "bias": scatter_about(arg_keys[4], (HID,), 0.5, 3.0, (), jnp.float32),
        "requests": draw_requests(jax.random.fold_in(arg_keys[13], 71), 0),
        "cross_peer": draw_cross_peer(jax.random.fold_in(arg_keys[13], 71), 0),
        "cross_block": draw_cross_block(jax.random.fold_in(arg_keys[13], 71), 0),
        "cross_count": draw_cross_count(jax.random.fold_in(arg_keys[13], 71), 0),
        "cross_w": scatter_about(arg_keys[9], (CROSS, BLK, BLK), (4 * BLK) ** -0.5, 0.25, ((0, 8),)),
        "inner_src": plant(jax.random.randint(arg_keys[10], (INNER,), 0, NB), jax.random.fold_in(arg_keys[10], 1), 0, NB - 1).astype(jnp.int32),
        "inner_dst": plant(jax.random.randint(arg_keys[11], (INNER,), 0, NB), jax.random.fold_in(arg_keys[11], 1), 0, NB - 1).astype(jnp.int32),
        "inner_w": scatter_about(arg_keys[12], (INNER, BLK, BLK), (4 * BLK) ** -0.5, 0.25, ((0, 8),)),
    }


HIGH = lax.Precision.HIGHEST

def aggregate(blocks, requests, cross_peer, cross_block, cross_count, cross_w, inner_src, inner_dst, inner_w, backward):

    def per_part(totals, owner):
        tile_w = lax.dynamic_slice_in_dim(cross_w, owner * CT, CT, 0).astype(jnp.float32)
        far_part = lax.dynamic_slice_in_dim(cross_peer, owner * CT, CT, 0)
        near = owner * NB + lax.dynamic_slice_in_dim(cross_block, owner * CT, CT, 0)
        far = far_part * NB + requests[far_part, owner]
        living = (jnp.arange(CT, dtype=jnp.int32) < cross_count[owner]).astype(jnp.float32)[:, None, None]
        into_near = jnp.einsum('kfj,kij->kfi', blocks[far].astype(jnp.float32), tile_w, precision=HIGH)
        into_far = jnp.einsum('kfi,kij->kfj', blocks[near].astype(jnp.float32), tile_w, precision=HIGH)
        totals = totals.at[near].add(into_near * living)
        totals = totals.at[far].add(into_far * living)
        inner_tiles = lax.dynamic_slice_in_dim(inner_w, owner * IT, IT, 0).astype(jnp.float32)
        anchor = owner * NB + lax.dynamic_slice_in_dim(inner_src, owner * IT, IT, 0)
        target = owner * NB + lax.dynamic_slice_in_dim(inner_dst, owner * IT, IT, 0)
        if backward:
            moved = jnp.einsum('kfi,kij->kfj', blocks[target].astype(jnp.float32), inner_tiles, precision=HIGH)
            totals = totals.at[anchor].add(moved)
        else:
            moved = jnp.einsum('kfj,kij->kfi', blocks[anchor].astype(jnp.float32), inner_tiles, precision=HIGH)
            totals = totals.at[target].add(moved)
        return (totals, None)
    start = jnp.zeros(blocks.shape, jnp.float32)
    return lax.scan(per_part, start, jnp.arange(N_DOM, dtype=jnp.int32))[0]

def reference(feats, grad_out, w_self, w_neigh, bias, requests, cross_peer, cross_block, cross_count, cross_w, inner_src, inner_dst, inner_w):

    def apply_graph(field, backward):
        blocks = field.reshape(F, N_DOM * NB, BLK).transpose(1, 0, 2)
        summed = aggregate(blocks, requests, cross_peer, cross_block, cross_count, cross_w, inner_src, inner_dst, inner_w, backward)
        return summed.transpose(1, 0, 2).reshape(F, NODES)
    neighbor = apply_graph(feats, False).astype(jnp.bfloat16)
    preact = jnp.dot(w_self.T, feats, preferred_element_type=jnp.float32)
    preact = preact + jnp.dot(w_neigh.T, neighbor, preferred_element_type=jnp.float32) + bias[:, None]
    sigmoid_z = jax.nn.sigmoid(preact)
    activated = (preact * sigmoid_z).astype(jnp.bfloat16)
    slope = (grad_out.astype(jnp.float32) * sigmoid_z * (1.0 + preact * (1.0 - sigmoid_z))).astype(jnp.bfloat16)
    norm_scale = 1.0 / math.sqrt(NODES)
    grad_self = jnp.dot(feats, slope.T, preferred_element_type=jnp.float32) * norm_scale
    grad_neigh = jnp.dot(neighbor, slope.T, preferred_element_type=jnp.float32) * norm_scale
    grad_bias = lax.optimization_barrier(jnp.sum(slope.astype(jnp.float32), axis=1)) * norm_scale
    back_agg = jnp.dot(w_neigh, slope, preferred_element_type=jnp.float32).astype(jnp.bfloat16)
    d_feats = (jnp.dot(w_self, slope, preferred_element_type=jnp.float32) + apply_graph(back_agg, True)).astype(jnp.bfloat16)
    return (activated, d_feats, grad_self, grad_neigh, grad_bias)
```

```python
import functools
import math

import jax
import jax.numpy as jnp
from jax import lax
from jax.experimental import pallas as pl
from jax.experimental.pallas import tpu as pltpu
from jax.sharding import PartitionSpec as P

MESH = pl.DeviceIdType.MESH
F32 = jnp.float32
BF16 = jnp.bfloat16


def each(first, count, step):
    if count <= 16:
        for i in range(first, count):
            step(i)
    else:

        def body(i, carry):
            step(i)
            return carry

        lax.fori_loop(first, count, body, 0)


def grouped(count, group, step):
    while count % group:
        group //= 2

    def body(i, carry):
        step([i * group + u for u in range(group)])
        return carry

    lax.fori_loop(0, count // group, body, 0)


def layer_kernel(
    sizes,
    links_ref,
    wanted_ref,
    peer_ref,
    block_ref,
    src_ref,
    dst_ref,
    feats_ref,
    gout_ref,
    wself_ref,
    wneigh_ref,
    bias_ref,
    cross_hbm,
    inner_hbm,
    act_ref,
    dfeats_ref,
    gself_ref,
    gneigh_ref,
    gbias_ref,
    cross_v,
    inner_v,
    far_send,
    far_recv_fwd,
    far_recv_bwd,
    out_send,
    ret_recv,
    chain,
    peer_chain,
    field,
    nbr,
    back,
    self_term,
    feats_n,
    gout_n,
    nbr_n,
    slope_n,
    act_n,
    back_n,
    self_n,
    grad_send,
    grad_recv,
    red_send,
    red_recv,
    red_all,
    load_sems,
    far_ss,
    far_rs,
    ret_ss,
    ret_rs,
    rep_ss,
    rep_rs,
    red_ss,
    red_rs,
    all_ss,
    all_rs,
):
    doms, reps, ct, it, nb, blk, cols, scale = sizes
    far_recv = (far_recv_fwd, far_recv_bwd)
    entries = it + ct + doms
    channels = cols * reps
    part = nb * blk // reps
    d = lax.axis_index("dom")
    r = lax.axis_index("rep")

    load_cross = pltpu.make_async_copy(cross_hbm, cross_v, load_sems.at[0])
    load_inner = pltpu.make_async_copy(inner_hbm, inner_v, load_sems.at[1])
    load_cross.start()
    load_inner.start()

    def dom_at(o):
        return lax.rem(d + o, doms)

    def rep_at(o):
        return lax.rem(r + o, reps)

    barrier = pltpu.get_barrier_semaphore()
    each(
        1,
        doms,
        lambda o: pl.semaphore_signal(
            barrier, inc=1, device_id={"dom": dom_at(o)}, device_id_type=MESH
        ),
    )
    each(
        1,
        reps,
        lambda o: pl.semaphore_signal(
            barrier, inc=1, device_id={"rep": rep_at(o)}, device_id_type=MESH
        ),
    )

    def lanes(i, width):
        return pl.ds(pl.multiple_of(i * width, width), width)

    def rows(i, height):
        return pl.ds(pl.multiple_of(i * height, height), height)

    def stage_far(turn, field):
        def stage(q):
            far_send[turn, q] = field[jnp.maximum(wanted_ref[0, q], 0)]

        each(0, doms, stage)
        far_recv[turn][d] = jnp.zeros((cols, blk), BF16)

    def far_copy(turn, o):
        q = dom_at(o)
        return pltpu.make_async_remote_copy(
            src_ref=far_send.at[turn, q],
            dst_ref=far_recv[turn].at[d],
            send_sem=far_ss.at[turn, o],
            recv_sem=far_rs.at[turn, o],
            device_id={"dom": q},
            device_id_type=MESH,
        )

    def ret_copy(turn, o):
        q = dom_at(o)
        return pltpu.make_async_remote_copy(
            src_ref=out_send.at[turn, q],
            dst_ref=ret_recv.at[turn, d],
            send_sem=ret_ss.at[turn, o],
            recv_sem=ret_rs.at[turn, o],
            device_id={"dom": q},
            device_id_type=MESH,
        )

    def to_nodes(slot, source, target, o):
        q = rep_at(o)
        return pltpu.make_async_remote_copy(
            src_ref=source.at[:, lanes(q, part)],
            dst_ref=target.at[rows(r, cols), :],
            send_sem=rep_ss.at[slot, o],
            recv_sem=rep_rs.at[slot, o],
            device_id={"rep": q},
            device_id_type=MESH,
        )

    def to_channels(slot, source, target, o):
        q = rep_at(o)
        return pltpu.make_async_remote_copy(
            src_ref=source.at[rows(q, cols), :],
            dst_ref=target.at[:, lanes(r, part)],
            send_sem=rep_ss.at[slot, o],
            recv_sem=rep_rs.at[slot, o],
            device_id={"rep": q},
            device_id_type=MESH,
        )

    def start_nodes(slot, source, target):
        each(1, reps, lambda o: to_nodes(slot, source, target, o).start())
        target[rows(r, cols), :] = source[:, lanes(r, part)]

    def wait_nodes(slot, source, target):
        each(1, reps, lambda o: to_nodes(slot, source, target, o).wait())

    def start_channels(slot, source, target):
        each(1, reps, lambda o: to_channels(slot, source, target, o).start())
        target[:, lanes(r, part)] = source[rows(r, cols), :]

    def wait_channels(slot, source, target):
        each(1, reps, lambda o: to_channels(slot, source, target, o).wait())

    def times(x, w):
        return jnp.dot(x, w, preferred_element_type=F32)

    def times_t(x, w):
        return lax.dot_general(x, w, (((1,), (1,)), ((), ())), preferred_element_type=F32)

    def add_peers(turn, field):
        def step(ks):
            moved = [times(field[block_ref[k]], cross_v[k]) for k in ks]
            for k, value in zip(ks, moved):
                peer_chain[k + 1] = peer_chain[links_ref[2, k]] + value

        grouped(ct, 8, step)

        def stage(q):
            out_send[turn, q] = peer_chain[links_ref[2, entries + q]]

        each(0, doms, stage)
        ret_recv[turn, d] = jnp.zeros((cols, blk), F32)
        each(1, doms, lambda o: ret_copy(turn, o).start())

    def add_inner(turn, field):
        def step(ks):
            if turn == 0:
                moved = [times_t(field[src_ref[k]], inner_v[k]) for k in ks]
            else:
                moved = [times(field[dst_ref[k]], inner_v[k]) for k in ks]
            for k, value in zip(ks, moved):
                chain[k + 1] = chain[links_ref[turn, k]] + value

        grouped(it, 8, step)

    def add_near(turn):
        def step(ks):
            moved = [times_t(far_recv[turn][peer_ref[k]], cross_v[k]) for k in ks]
            for k, value in zip(ks, moved):
                chain[it + k + 1] = chain[links_ref[turn, it + k]] + value

        grouped(ct, 8, step)

    def add_returned(turn):
        each(1, doms, lambda o: ret_copy(turn, o).wait())

        def step(q):
            e = it + ct + q
            chain[e + 1] = chain[links_ref[turn, e]] + ret_recv[turn, q]

        each(0, doms, step)

    chain[0] = jnp.zeros((cols, blk), F32)
    peer_chain[0] = jnp.zeros((cols, blk), F32)
    for b in range(nb):
        field[b] = feats_ref[:, b * blk : (b + 1) * blk]
    stage_far(0, field)
    pl.semaphore_wait(barrier, doms - 1 + reps - 1)
    each(1, doms, lambda o: far_copy(0, o).start())
    start_nodes(0, feats_ref, feats_n)
    start_nodes(1, gout_ref, gout_n)

    load_cross.wait()
    add_peers(0, field)
    load_inner.wait()
    add_inner(0, field)
    each(1, doms, lambda o: far_copy(0, o).wait())
    add_near(0)
    add_returned(0)
    for b in range(nb):
        nbr[:, b * blk : (b + 1) * blk] = chain[links_ref[0, entries + b]].astype(BF16)
    start_nodes(2, nbr, nbr_n)

    def back_copy(o):
        q = rep_at(o)
        return pltpu.make_async_remote_copy(
            src_ref=back_n.at[q],
            dst_ref=back.at[rows(r, nb // reps)],
            send_sem=rep_ss.at[3, o],
            recv_sem=rep_rs.at[3, o],
            device_id={"rep": q},
            device_id_type=MESH,
        )

    wide = min(256, part)
    bias_cols = jnp.transpose(jnp.broadcast_to(bias_ref[...], (blk, channels)))
    bias_cols = jnp.concatenate([bias_cols] * (wide // blk), axis=1)
    wself_t = jnp.transpose(wself_ref[...].astype(F32)).astype(BF16)
    wneigh_t = jnp.transpose(wneigh_ref[...].astype(F32)).astype(BF16)
    wait_nodes(0, feats_ref, feats_n)
    wait_nodes(1, gout_ref, gout_n)
    wait_nodes(2, nbr, nbr_n)
    for c in range(part // wide):
        at = slice(c * wide, (c + 1) * wide)
        preact = times(wself_t, feats_n[:, at]) + times(wneigh_t, nbr_n[:, at]) + bias_cols
        s = jax.nn.sigmoid(preact)
        act_n[:, at] = (preact * s).astype(BF16)
        slope = (gout_n[:, at].astype(F32) * s * (1.0 + preact * (1.0 - s))).astype(BF16)
        slope_n[:, at] = slope
        mixed = times(wneigh_ref[...], slope).astype(BF16)
        for q in range(reps):
            for u in range(wide // blk):
                back_n[q, c * (wide // blk) + u] = mixed[
                    q * cols : (q + 1) * cols, u * blk : (u + 1) * blk
                ]
    each(1, reps, lambda o: back_copy(o).start())
    back[rows(r, nb // reps)] = back_n[r]
    self_n[...] = times(wself_ref[...], slope_n[...]).astype(BF16)
    slope = slope_n[...]
    grads = (times_t(feats_n[...], slope), times_t(nbr_n[...], slope))
    ones = times_t(jnp.ones((16, part), BF16), slope)[:8]
    tall = 2 * cols + 8
    for q in range(reps):
        for i, grad in enumerate(grads):
            grad_send[q, i * cols : (i + 1) * cols] = grad[q * cols : (q + 1) * cols]
        grad_send[q, 2 * cols :] = ones

    def grad_copy(o):
        q = rep_at(o)
        return pltpu.make_async_remote_copy(
            src_ref=grad_send.at[q],
            dst_ref=grad_recv.at[r],
            send_sem=rep_ss.at[6, o],
            recv_sem=rep_rs.at[6, o],
            device_id={"rep": q},
            device_id_type=MESH,
        )

    each(1, reps, lambda o: back_copy(o).wait())
    stage_far(1, back)
    each(1, doms, lambda o: far_copy(1, o).start())
    each(1, reps, lambda o: grad_copy(o).start())
    grad_recv[r] = grad_send[r]
    add_peers(1, back)
    start_channels(4, self_n, self_term)
    start_channels(5, act_n, act_ref)

    add_inner(1, back)

    short = 2 * cols // doms
    split = short % 8 == 0 and short > 0
    each(1, reps, lambda o: grad_copy(o).wait())
    total = grad_recv[0]
    for q in range(1, reps):
        total = total + grad_recv[q]

    def red_copy(o):
        q = dom_at(o)
        return pltpu.make_async_remote_copy(
            src_ref=red_send.at[q] if split else red_send.at[0],
            dst_ref=red_recv.at[d],
            send_sem=red_ss.at[o],
            recv_sem=red_rs.at[o],
            device_id={"dom": q},
            device_id_type=MESH,
        )

    def all_copy(o):
        mine = red_all.at[rows(d, short), :]
        return pltpu.make_async_remote_copy(
            src_ref=mine,
            dst_ref=mine,
            send_sem=all_ss.at[o],
            recv_sem=all_rs.at[o],
            device_id={"dom": dom_at(o)},
            device_id_type=MESH,
        )

    if split:
        for q in range(doms):
            red_send[q, :short] = total[q * short : (q + 1) * short]
            red_send[q, short:] = total[2 * cols :]
        red_recv[d] = red_send[d]
    else:
        red_send[0] = total
        red_recv[d] = total
    each(1, doms, lambda o: red_copy(o).start())

    each(1, doms, lambda o: far_copy(1, o).wait())
    add_near(1)

    each(1, doms, lambda o: red_copy(o).wait())
    height = short + 8 if split else tall
    total = lax.fori_loop(
        0, doms, lambda q, acc: acc + red_recv[q], jnp.zeros((height, channels), F32)
    )
    gbias_ref[...] = total[height - 8 :] * scale
    if split:
        red_all[rows(d, short), :] = total[:short]
        each(1, doms, lambda o: all_copy(o).start())
    else:
        red_all[...] = total[: 2 * cols]

    add_returned(1)
    wait_channels(4, self_n, self_term)
    for b in range(nb):
        at = slice(b * blk, (b + 1) * blk)
        dfeats_ref[:, at] = (
            self_term[:, at].astype(F32) + chain[links_ref[1, entries + b]]
        ).astype(BF16)
    wait_channels(5, act_n, act_ref)
    if split:
        each(1, doms, lambda o: all_copy(o).wait())
    gself_ref[...] = red_all[:cols] * scale
    gneigh_ref[...] = red_all[cols:] * scale


def local(
    feats,
    grad_out,
    w_self,
    w_neigh,
    bias,
    requests,
    cross_peer,
    cross_block,
    cross_count,
    cross_w,
    inner_src,
    inner_dst,
    inner_w,
):
    cols, node_count = feats.shape
    ct, blk = cross_w.shape[:2]
    it = inner_w.shape[0]
    nb = node_count // blk
    doms = lax.axis_size("dom")
    reps = lax.axis_size("rep")
    channels = w_self.shape[1]
    part = node_count // reps
    scale = 1.0 / math.sqrt(node_count * doms)
    wanted = requests[0]

    entries = it + ct + doms
    live = jnp.arange(ct, dtype=jnp.int32) < cross_count[0]
    near = jnp.where(live, cross_block, -1)
    keys = jnp.stack(
        [
            jnp.concatenate([inner_dst, near, wanted]),
            jnp.concatenate([inner_src, near, wanted]),
            jnp.concatenate(
                [jnp.where(live, cross_peer, -1), jnp.full((it + doms,), -1, jnp.int32)]
            ),
        ]
    )
    ends = max(nb, doms)
    asked = jnp.concatenate(
        [keys, jnp.broadcast_to(jnp.arange(ends, dtype=jnp.int32), (3, ends))], axis=1
    )
    place = jnp.arange(entries, dtype=jnp.int32)
    limit = jnp.minimum(jnp.arange(entries + ends, dtype=jnp.int32), entries)
    same = (keys[:, None, :] == asked[:, :, None]) & (place[None, None, :] < limit[None, :, None])
    links = jnp.max(jnp.where(same, place[None, None, :] + 1, 0), axis=2)

    short = 2 * cols // doms
    split = short % 8 == 0 and short > 0
    red_rows = short + 8 if split else 2 * cols + 8
    smem = pl.BlockSpec(memory_space=pltpu.SMEM)
    vmem = pl.BlockSpec(memory_space=pltpu.VMEM)
    hbm = pl.BlockSpec(memory_space=pl.ANY)
    dma = pltpu.SemaphoreType.DMA
    act, dfeats, gself, gneigh, gbias = pl.pallas_call(
        functools.partial(layer_kernel, (doms, reps, ct, it, nb, blk, cols, scale)),
        out_shape=(
            jax.ShapeDtypeStruct((cols, node_count), BF16),
            jax.ShapeDtypeStruct((cols, node_count), BF16),
            jax.ShapeDtypeStruct((cols, channels), F32),
            jax.ShapeDtypeStruct((cols, channels), F32),
            jax.ShapeDtypeStruct((8, channels), F32),
        ),
        in_specs=[smem] * 6 + [vmem] * 5 + [hbm] * 2,
        out_specs=(vmem,) * 5,
        scratch_shapes=[
            pltpu.VMEM((ct, blk, blk), BF16),
            pltpu.VMEM((it, blk, blk), BF16),
            pltpu.VMEM((2, doms, cols, blk), BF16),
            pltpu.VMEM((doms, cols, blk), BF16),
            pltpu.VMEM((doms, cols, blk), BF16),
            pltpu.VMEM((2, doms, cols, blk), F32),
            pltpu.VMEM((2, doms, cols, blk), F32),
            pltpu.VMEM((entries + 1, cols, blk), F32),
            pltpu.VMEM((ct + 1, cols, blk), F32),
            pltpu.VMEM((nb, cols, blk), BF16),
            pltpu.VMEM((cols, node_count), BF16),
            pltpu.VMEM((nb, cols, blk), BF16),
            pltpu.VMEM((cols, node_count), BF16),
            pltpu.VMEM((channels, part), BF16),
            pltpu.VMEM((channels, part), BF16),
            pltpu.VMEM((channels, part), BF16),
            pltpu.VMEM((channels, part), BF16),
            pltpu.VMEM((channels, part), BF16),
            pltpu.VMEM((reps, nb // reps, cols, blk), BF16),
            pltpu.VMEM((channels, part), BF16),
            pltpu.VMEM((reps, 2 * cols + 8, channels), F32),
            pltpu.VMEM((reps, 2 * cols + 8, channels), F32),
            pltpu.VMEM((doms if split else 1, red_rows, channels), F32),
            pltpu.VMEM((doms, red_rows, channels), F32),
            pltpu.VMEM((2 * cols, channels), F32),
            dma((2,)),
            dma((2, doms)),
            dma((2, doms)),
            dma((2, doms)),
            dma((2, doms)),
            dma((7, reps)),
            dma((7, reps)),
            dma((doms,)),
            dma((doms,)),
            dma((doms,)),
            dma((doms,)),
        ],
        compiler_params=pltpu.CompilerParams(
            collective_id=0, has_side_effects=True, vmem_limit_bytes=40 * 1024 * 1024
        ),
    )(
        links,
        requests,
        cross_peer,
        cross_block,
        inner_src,
        inner_dst,
        feats,
        grad_out,
        w_self,
        w_neigh,
        bias.reshape(1, channels),
        cross_w,
        inner_w,
    )
    out_rows = channels // reps
    grad_bias = lax.dynamic_slice_in_dim(gbias[0], lax.axis_index("rep") * out_rows, out_rows, 0)
    return act, dfeats, gself, gneigh, grad_bias


def solution(mesh):
    placed = (
        P("rep", "dom"),
        P("rep", "dom"),
        P(),
        P(),
        P(),
        P("dom", None),
        P("dom"),
        P("dom"),
        P("dom"),
        P("dom", None, None),
        P("dom"),
        P("dom"),
        P("dom", None, None),
    )
    return jax.shard_map(
        local,
        mesh=mesh,
        in_specs=placed,
        out_specs=(P("rep", "dom"), P("rep", "dom"), P("rep", None), P("rep", None), P("rep")),
        check_vma=False,
    )
```

```python
import functools
import math

import jax
import jax.numpy as jnp
from jax import lax
from jax.experimental import pallas as pl
from jax.experimental.pallas import tpu as pltpu
from jax.sharding import PartitionSpec as P

MESH = pl.DeviceIdType.MESH
F32 = jnp.float32
BF16 = jnp.bfloat16
GROUP = 32
LOADS = 12


def each(first, count, step):
    if count <= 16:
        for i in range(first, count):
            step(i)
    else:

        def body(i, carry):
            step(i)
            return carry

        lax.fori_loop(first, count, body, 0)


def grouped(count, group, step):
    while count % group:
        group //= 2

    def body(i, carry):
        step([i * group + u for u in range(group)])
        return carry

    lax.fori_loop(0, count // group, body, 0)


def layer_kernel(
    sizes,
    links_ref,
    feats_hbm,
    gout_hbm,
    wself_hbm,
    wneigh_hbm,
    bias_hbm,
    cross_hbm,
    inner_hbm,
    field_out,
    grad_out,
    feats_ref,
    wself_ref,
    wneigh_ref,
    bias_ref,
    cross_v,
    inner_v,
    far_send,
    far_recv_fwd,
    far_recv_bwd,
    out_send,
    ret_recv,
    chain,
    peer_chain,
    field,
    nbr,
    back,
    self_term,
    feats_n,
    gout_n,
    nbr_n,
    slope_n,
    act_n,
    back_n,
    self_n,
    grad_send,
    grad_recv,
    red_send,
    red_recv,
    red_all,
    load_sems,
    big_sems,
    far_ss,
    far_rs,
    ret_ss,
    ret_rs,
    rep_ss,
    rep_rs,
    red_ss,
    red_rs,
    all_ss,
    all_rs,
):
    doms, reps, ct, it, nb, blk, cols, scale = sizes
    far_recv = (far_recv_fwd, far_recv_bwd)
    entries = it + ct + doms
    channels = cols * reps
    part = nb * blk // reps
    d = lax.axis_index("dom")
    r = lax.axis_index("rep")


    def dom_at(o):
        return lax.rem(d + o, doms)

    def rep_at(o):
        return lax.rem(r + o, reps)

    barrier = pltpu.get_barrier_semaphore()
    each(
        1,
        doms,
        lambda o: pl.semaphore_signal(
            barrier, inc=1, device_id={"dom": dom_at(o)}, device_id_type=MESH
        ),
    )
    each(
        1,
        reps,
        lambda o: pl.semaphore_signal(
            barrier, inc=1, device_id={"rep": rep_at(o)}, device_id_type=MESH
        ),
    )

    def lanes(i, width):
        return pl.ds(pl.multiple_of(i * width, width), width)

    def rows(i, height):
        return pl.ds(pl.multiple_of(i * height, height), height)

    pairs = (
        (feats_hbm, feats_ref),
        (gout_hbm.at[:, lanes(r, part)], gout_n.at[rows(r, cols), :]),
        (wself_hbm, wself_ref),
        (wneigh_hbm, wneigh_ref),
        (bias_hbm, bias_ref),
    )
    loads = [
        pltpu.make_async_copy(source, target, load_sems.at[i])
        for i, (source, target) in enumerate(pairs)
    ]
    loads[0].start()
    bulk = ct // LOADS
    big = [
        pltpu.make_async_copy(
            cross_hbm.at[pl.ds(i * bulk, bulk)],
            cross_v.at[pl.ds(i * bulk, bulk)],
            big_sems.at[i],
        )
        for i in range(LOADS)
    ]
    big.append(pltpu.make_async_copy(inner_hbm, inner_v, big_sems.at[LOADS]))
    for load in big + loads[1:]:
        load.start()
    last = entries + max(nb, doms)
    act_ref = field_out.at[0]
    dfeats_ref = field_out.at[1]

    def stage_far(turn, field):
        def stage(q):
            far_send[turn, q] = field[links_ref[0, last + it + ct + q]]

        each(0, doms, stage)
        far_recv[turn][d] = jnp.zeros((cols, blk), BF16)

    def far_copy(turn, o):
        q = dom_at(o)
        return pltpu.make_async_remote_copy(
            src_ref=far_send.at[turn, q],
            dst_ref=far_recv[turn].at[d],
            send_sem=far_ss.at[turn, o],
            recv_sem=far_rs.at[turn, o],
            device_id={"dom": q},
            device_id_type=MESH,
        )

    def ret_copy(turn, o):
        q = dom_at(o)
        return pltpu.make_async_remote_copy(
            src_ref=out_send.at[turn, q],
            dst_ref=ret_recv.at[turn, d],
            send_sem=ret_ss.at[turn, o],
            recv_sem=ret_rs.at[turn, o],
            device_id={"dom": q},
            device_id_type=MESH,
        )

    def to_nodes(slot, source, target, o):
        q = rep_at(o)
        return pltpu.make_async_remote_copy(
            src_ref=source.at[:, lanes(q, part)],
            dst_ref=target.at[rows(r, cols), :],
            send_sem=rep_ss.at[slot, o],
            recv_sem=rep_rs.at[slot, o],
            device_id={"rep": q},
            device_id_type=MESH,
        )

    def to_channels(slot, source, target, o):
        q = rep_at(o)
        return pltpu.make_async_remote_copy(
            src_ref=source.at[rows(q, cols), :],
            dst_ref=target.at[:, lanes(r, part)],
            send_sem=rep_ss.at[slot, o],
            recv_sem=rep_rs.at[slot, o],
            device_id={"rep": q},
            device_id_type=MESH,
        )

    def start_nodes(slot, source, target):
        each(1, reps, lambda o: to_nodes(slot, source, target, o).start())
        target[rows(r, cols), :] = source[:, lanes(r, part)]

    def wait_nodes(slot, source, target):
        each(1, reps, lambda o: to_nodes(slot, source, target, o).wait())

    def start_channels(slot, source, target):
        each(1, reps, lambda o: to_channels(slot, source, target, o).start())
        target[:, lanes(r, part)] = source[rows(r, cols), :]

    def wait_channels(slot, source, target):
        each(1, reps, lambda o: to_channels(slot, source, target, o).wait())

    def times(x, w):
        return jnp.dot(x, w, preferred_element_type=F32)

    def times_t(x, w):
        return lax.dot_general(x, w, (((1,), (1,)), ((), ())), preferred_element_type=F32)

    def add_peers(turn, field):
        def step(ks):
            moved = [times(field[links_ref[0, last + it + k]], cross_v[k]) for k in ks]
            for k, value in zip(ks, moved):
                peer_chain[k + 1] = peer_chain[links_ref[2, k]] + value

        grouped(ct, GROUP, step)

        def stage(q):
            out_send[turn, q] = peer_chain[links_ref[2, entries + q]]

        each(0, doms, stage)
        ret_recv[turn, d] = jnp.zeros((cols, blk), F32)
        each(1, doms, lambda o: ret_copy(turn, o).start())

    def add_inner(turn, field):
        def step(ks):
            if turn == 0:
                moved = [times_t(field[links_ref[1, last + k]], inner_v[k]) for k in ks]
            else:
                moved = [times(field[links_ref[0, last + k]], inner_v[k]) for k in ks]
            for k, value in zip(ks, moved):
                chain[k + 1] = chain[links_ref[turn, k]] + value

        grouped(it, 16, step)

    def add_near(turn):
        def step(ks):
            moved = [times_t(far_recv[turn][links_ref[2, last + k]], cross_v[k]) for k in ks]
            for k, value in zip(ks, moved):
                chain[it + k + 1] = chain[links_ref[turn, it + k]] + value

        grouped(ct, GROUP, step)

    def add_returned(turn):
        each(1, doms, lambda o: ret_copy(turn, o).wait())

        def step(q):
            e = it + ct + q
            chain[e + 1] = chain[links_ref[turn, e]] + ret_recv[turn, q]

        each(0, doms, step)

    chain[0] = jnp.zeros((cols, blk), F32)
    peer_chain[0] = jnp.zeros((cols, blk), F32)
    loads[0].wait()
    for b in range(nb):
        field[b] = feats_ref[:, b * blk : (b + 1) * blk]
    stage_far(0, field)
    pl.semaphore_wait(barrier, doms - 1 + reps - 1)
    each(1, doms, lambda o: far_copy(0, o).start())
    start_nodes(0, feats_ref, feats_n)
    each(1, reps, lambda o: to_nodes(1, gout_hbm, gout_n, o).start())

    for load in big[:-1]:
        load.wait()
    add_peers(0, field)
    big[-1].wait()
    add_inner(0, field)
    each(1, doms, lambda o: far_copy(0, o).wait())
    add_near(0)
    add_returned(0)
    for b in range(nb):
        nbr[:, b * blk : (b + 1) * blk] = chain[links_ref[0, entries + b]].astype(BF16)
    start_nodes(2, nbr, nbr_n)

    wide = min(256, part)
    step_blocks = wide // blk

    def back_copy(c, o):
        q = rep_at(o)
        first = pl.multiple_of(r * (nb // reps) + c * step_blocks, step_blocks)
        return pltpu.make_async_remote_copy(
            src_ref=back_n.at[q, pl.ds(c * step_blocks, step_blocks)],
            dst_ref=back.at[pl.ds(first, step_blocks)],
            send_sem=rep_ss.at[7 + c, o],
            recv_sem=rep_rs.at[7 + c, o],
            device_id={"rep": q},
            device_id_type=MESH,
        )

    for load in loads[1:]:
        load.wait()
    bias_cols = jnp.transpose(jnp.broadcast_to(bias_ref[...], (blk, channels)))
    bias_cols = jnp.concatenate([bias_cols] * (wide // blk), axis=1)
    wself_t = jnp.transpose(wself_ref[...].astype(F32)).astype(BF16)
    wneigh_t = jnp.transpose(wneigh_ref[...].astype(F32)).astype(BF16)
    wait_nodes(0, feats_ref, feats_n)
    wait_nodes(1, gout_hbm, gout_n)
    wait_nodes(2, nbr, nbr_n)
    for c in range(part // wide):
        at = slice(c * wide, (c + 1) * wide)
        preact = times(wself_t, feats_n[:, at]) + times(wneigh_t, nbr_n[:, at]) + bias_cols
        s = jax.nn.sigmoid(preact)
        act_n[:, at] = (preact * s).astype(BF16)
        slope = (gout_n[:, at].astype(F32) * s * (1.0 + preact * (1.0 - s))).astype(BF16)
        slope_n[:, at] = slope
        mixed = times(wneigh_ref[...], slope).astype(BF16)
        for q in range(reps):
            for u in range(wide // blk):
                back_n[q, c * (wide // blk) + u] = mixed[
                    q * cols : (q + 1) * cols, u * blk : (u + 1) * blk
                ]
        each(1, reps, lambda o: back_copy(c, o).start())
    back[rows(r, nb // reps)] = back_n[r]
    slope = slope_n[...]
    grads = (times_t(feats_n[...], slope), times_t(nbr_n[...], slope))
    ones = times_t(jnp.ones((16, part), BF16), slope)[:8]
    tall = 2 * cols + 8
    for q in range(reps):
        for i, grad in enumerate(grads):
            grad_send[q, i * cols : (i + 1) * cols] = grad[q * cols : (q + 1) * cols]
        grad_send[q, 2 * cols :] = ones

    def grad_copy(o):
        q = rep_at(o)
        return pltpu.make_async_remote_copy(
            src_ref=grad_send.at[q],
            dst_ref=grad_recv.at[r],
            send_sem=rep_ss.at[6, o],
            recv_sem=rep_rs.at[6, o],
            device_id={"rep": q},
            device_id_type=MESH,
        )

    each(1, reps, lambda o: grad_copy(o).start())
    grad_recv[r] = grad_send[r]
    self_n[...] = times(wself_ref[...], slope).astype(BF16)
    for c in range(part // wide):
        each(1, reps, lambda o: back_copy(c, o).wait())
    stage_far(1, back)
    each(1, doms, lambda o: far_copy(1, o).start())
    short = 2 * cols // doms
    split = short % 8 == 0 and short > 0
    each(1, reps, lambda o: grad_copy(o).wait())
    total = grad_recv[0]
    for q in range(1, reps):
        total = total + grad_recv[q]

    def red_copy(o):
        q = dom_at(o)
        return pltpu.make_async_remote_copy(
            src_ref=red_send.at[q] if split else red_send.at[0],
            dst_ref=red_recv.at[d],
            send_sem=red_ss.at[o],
            recv_sem=red_rs.at[o],
            device_id={"dom": q},
            device_id_type=MESH,
        )

    def all_copy(o):
        mine = red_all.at[rows(d, short), :]
        return pltpu.make_async_remote_copy(
            src_ref=mine,
            dst_ref=mine,
            send_sem=all_ss.at[o],
            recv_sem=all_rs.at[o],
            device_id={"dom": dom_at(o)},
            device_id_type=MESH,
        )

    if split:
        for q in range(doms):
            red_send[q, :short] = total[q * short : (q + 1) * short]
            red_send[q, short:] = total[2 * cols :]
        red_recv[d] = red_send[d]
    else:
        red_send[0] = total
        red_recv[d] = total
    each(1, doms, lambda o: red_copy(o).start())

    add_peers(1, back)
    start_channels(4, self_n, self_term)
    start_channels(5, act_n, act_ref)

    add_inner(1, back)
    each(1, doms, lambda o: red_copy(o).wait())
    height = short + 8 if split else tall
    total = lax.fori_loop(
        0, doms, lambda q, acc: acc + red_recv[q], jnp.zeros((height, channels), F32)
    )
    mine = pltpu.roll(total[height - 8 :], lax.rem(channels - r * cols, channels), 1)
    grad_out[2 * cols :] = mine * scale
    if split:
        red_all[rows(d, short), :] = total[:short]
        each(1, doms, lambda o: all_copy(o).start())
    else:
        red_all[...] = total[: 2 * cols]

    each(1, doms, lambda o: far_copy(1, o).wait())
    add_near(1)
    add_returned(1)
    wait_channels(4, self_n, self_term)
    for b in range(nb):
        at = slice(b * blk, (b + 1) * blk)
        dfeats_ref[:, at] = (
            self_term[:, at].astype(F32) + chain[links_ref[1, entries + b]]
        ).astype(BF16)
    wait_channels(5, act_n, act_ref)
    if split:
        each(1, doms, lambda o: all_copy(o).wait())
    grad_out[: 2 * cols] = red_all[...] * scale


def local(
    feats,
    grad_out,
    w_self,
    w_neigh,
    bias,
    requests,
    cross_peer,
    cross_block,
    cross_count,
    cross_w,
    inner_src,
    inner_dst,
    inner_w,
):
    cols, node_count = feats.shape
    ct, blk = cross_w.shape[:2]
    it = inner_w.shape[0]
    nb = node_count // blk
    doms = lax.axis_size("dom")
    reps = lax.axis_size("rep")
    channels = w_self.shape[1]
    part = node_count // reps
    scale = 1.0 / math.sqrt(node_count * doms)
    wanted = requests[0]

    entries = it + ct + doms
    live = jnp.arange(ct, dtype=jnp.int32) < cross_count[0]
    near = jnp.where(live, cross_block, -1)
    keys = jnp.stack(
        [
            jnp.concatenate([inner_dst, near, wanted]),
            jnp.concatenate([inner_src, near, wanted]),
            jnp.concatenate(
                [jnp.where(live, cross_peer, -1), jnp.full((it + doms,), -1, jnp.int32)]
            ),
        ]
    )
    ends = max(nb, doms)
    asked = jnp.concatenate(
        [keys, jnp.broadcast_to(jnp.arange(ends, dtype=jnp.int32), (3, ends))], axis=1
    )
    place = jnp.arange(entries, dtype=jnp.int32)
    limit = jnp.minimum(jnp.arange(entries + ends, dtype=jnp.int32), entries)
    same = (keys[:, None, :] == asked[:, :, None]) & (place[None, None, :] < limit[None, :, None])
    links = jnp.max(jnp.where(same, place[None, None, :] + 1, 0), axis=2)
    links = jnp.concatenate([links, jnp.maximum(keys, 0)], axis=1)

    short = 2 * cols // doms
    split = short % 8 == 0 and short > 0
    red_rows = short + 8 if split else 2 * cols + 8
    smem = pl.BlockSpec(memory_space=pltpu.SMEM)
    vmem = pl.BlockSpec(memory_space=pltpu.VMEM)
    hbm = pl.BlockSpec(memory_space=pl.ANY)
    dma = pltpu.SemaphoreType.DMA
    fields, grads = pl.pallas_call(
        functools.partial(layer_kernel, (doms, reps, ct, it, nb, blk, cols, scale)),
        out_shape=(
            jax.ShapeDtypeStruct((2, cols, node_count), BF16),
            jax.ShapeDtypeStruct((2 * cols + 8, channels), F32),
        ),
        in_specs=[smem] + [hbm] * 7,
        out_specs=(vmem,) * 2,
        scratch_shapes=[
            pltpu.VMEM((cols, node_count), BF16),
            pltpu.VMEM((channels, channels), BF16),
            pltpu.VMEM((channels, channels), BF16),
            pltpu.VMEM((1, channels), F32),
            pltpu.VMEM((ct, blk, blk), BF16),
            pltpu.VMEM((it, blk, blk), BF16),
            pltpu.VMEM((2, doms, cols, blk), BF16),
            pltpu.VMEM((doms, cols, blk), BF16),
            pltpu.VMEM((doms, cols, blk), BF16),
            pltpu.VMEM((2, doms, cols, blk), F32),
            pltpu.VMEM((2, doms, cols, blk), F32),
            pltpu.VMEM((entries + 1, cols, blk), F32),
            pltpu.VMEM((ct + 1, cols, blk), F32),
            pltpu.VMEM((nb, cols, blk), BF16),
            pltpu.VMEM((cols, node_count), BF16),
            pltpu.VMEM((nb, cols, blk), BF16),
            pltpu.VMEM((cols, node_count), BF16),
            pltpu.VMEM((channels, part), BF16),
            pltpu.VMEM((channels, part), BF16),
            pltpu.VMEM((channels, part), BF16),
            pltpu.VMEM((channels, part), BF16),
            pltpu.VMEM((channels, part), BF16),
            pltpu.VMEM((reps, nb // reps, cols, blk), BF16),
            pltpu.VMEM((channels, part), BF16),
            pltpu.VMEM((reps, 2 * cols + 8, channels), F32),
            pltpu.VMEM((reps, 2 * cols + 8, channels), F32),
            pltpu.VMEM((doms if split else 1, red_rows, channels), F32),
            pltpu.VMEM((doms, red_rows, channels), F32),
            pltpu.VMEM((2 * cols, channels), F32),
            dma((5,)),
            dma((LOADS + 1,)),
            dma((2, doms)),
            dma((2, doms)),
            dma((2, doms)),
            dma((2, doms)),
            dma((7 + part // min(256, part), reps)),
            dma((7 + part // min(256, part), reps)),
            dma((doms,)),
            dma((doms,)),
            dma((doms,)),
            dma((doms,)),
        ],
        compiler_params=pltpu.CompilerParams(
            collective_id=0, has_side_effects=True, vmem_limit_bytes=58 * 1024 * 1024
        ),
    )(
        links,
        feats,
        grad_out,
        w_self,
        w_neigh,
        bias.reshape(1, channels),
        cross_w,
        inner_w,
    )
    gself, gneigh = grads[:cols], grads[cols : 2 * cols]
    return fields[0], fields[1], gself, gneigh, grads[2 * cols, :cols]


def solution(mesh):
    placed = (
        P("rep", "dom"),
        P("rep", "dom"),
        P(),
        P(),
        P(),
        P("dom", None),
        P("dom"),
        P("dom"),
        P("dom"),
        P("dom", None, None),
        P("dom"),
        P("dom"),
        P("dom", None, None),
    )
    return jax.shard_map(
        local,
        mesh=mesh,
        in_specs=placed,
        out_specs=(P("rep", "dom"), P("rep", "dom"), P("rep", None), P("rep", None), P("rep")),
        check_vma=False,
    )
```
